32 devices in a mesh: grp: 4 (over y, x), dev: 8 (over z, core).
Axes of the slice: x: 2, y: 2, z: 4, core: 2. Of those that a mesh axis runs over, the one named last changes fastest.
Arguments:
- slab: bfloat16 [8, 8000, 8000], P('grp', 'dev'), may hold values from -2.5 to 2.5
- orbitals: bfloat16 [8000, 640], P('dev'), may hold values from -0.0625 to 0.0625
- hcore: float32 [8000, 8000], P('dev', 'grp'), may hold values from -6 to 6
- metric_inv: float32 [8, 8], replicated, may hold values from -1 to 2, as said below
Outputs:
- fock: float32 [8000, 8000], P('dev', 'grp')
The draws below stay inside these ranges and needn't reach their ends.
Inputs may be any that keep to these rules, and one draw needn't show every extreme that they name: `metric_inv`: symmetric.
All inputs are finite; a program needn't handle non-finite values.
Results may differ from the reference program's by a relative error of at most 0.0065.
Values may be sent and summed in bfloat16 or wider, within the bound.
A program may use at most 192 MiB of HBM per device.

```python
import math
import jax
import jax.numpy as jnp
from jax import lax

N = 8000
NOCC = 640
NAUX = 8


def draw_metric_inv(key, part):
    key_off, key_diag = jax.random.split(key)
    normal_draw = jnp.clip(jax.random.normal(key_off, (NAUX, NAUX), jnp.float32), -3.0, 3.0)
    symmetric = (normal_draw + normal_draw.T) * (0.3 / math.sqrt(NAUX))
    diag_values = jax.random.uniform(key_diag, (NAUX,), jnp.float32, 1.0, 1.5)
    identity = jnp.eye(NAUX, dtype=jnp.float32)
    return symmetric * (1.0 - identity) + identity * diag_values[None, :]


def spiked(drawn, own_key, source, target, shards_of, factor):
    def block_of(dim):
        return (jnp.arange(drawn.shape[dim]) // (drawn.shape[dim] // shards_of)).reshape((-1,) + (1,) * (drawn.ndim - 1 - dim))

    first = jax.random.permutation(own_key, shards_of)[block_of(target)]
    other_side = (block_of(target) + shards_of // 2) % shards_of
    return jnp.where((block_of(source) == first) | (block_of(source) == other_side), factor * drawn, drawn)


def level_of(own_key, shape, pieces, low, top_value):
    def one(dim, blocks):
        heights = jax.random.uniform(jax.random.fold_in(jax.random.fold_in(own_key, 6), dim), (blocks,), jnp.float32, low / len(pieces), top_value / len(pieces))
        return jnp.repeat(jnp.exp(heights), shape[dim] // blocks).reshape((-1,) + (1,) * (len(shape) - dim - 1))

    level = one(*pieces[0])
    for cut in pieces[1:]:
        level = level * one(*cut)
    return level


def bell_draw(rng, shape, width, bound, cuts=(), kind=jnp.bfloat16):
    gain = level_of(rng, shape, cuts, -0.22, 0.18) if cuts else 1.0
    values = jax.random.normal(rng, shape, jnp.float32) * width * gain
    return jnp.minimum(jnp.maximum(values, -bound), bound).astype(kind)


def noise_with(key, shape, width, limit, shards, heavy, held_as=jnp.bfloat16):
    entries = width * jax.random.normal(key, shape, jnp.float32)
    if shards:
        entries = entries * level_of(key, shape, shards, -0.22, 0.18)
    return jnp.clip(spiked(entries, jax.random.fold_in(key, 3), *heavy), -limit, limit).astype(held_as)


def setup_inputs(seed: int = 0) -> dict:
    streams_of = jax.random.split(jax.random.key(seed), 5)
    slab = noise_with(streams_of[0], (NAUX, N, N), 0.12, 2.5, ((0, 4), (1, 8)), (0, 2, 4, 2.0))
    orbitals = bell_draw(streams_of[1], (N, NOCC), N ** -0.5, 0.0625, ((0, 8),))
    hcore = bell_draw(streams_of[2], (N, N), 1.0, 6.0, ((0, 8), (1, 4)), jnp.float32)
    metric_inv = draw_metric_inv(jax.random.fold_in(streams_of[4], 71), 0)
    return dict(slab=slab, orbitals=orbitals, hcore=hcore, metric_inv=metric_inv)


def reference(slab, orbitals, hcore, metric_inv):
    half_done = jnp.stack([jnp.dot(slab[aux_index], orbitals, preferred_element_type=jnp.float32).astype(jnp.bfloat16) for aux_index in range(NAUX)])
    aux_density = jnp.sum(half_done.astype(jnp.float32) * orbitals.astype(jnp.float32)[None], axis=(1, 2))
    fit_coef = jnp.dot(metric_inv, aux_density, precision=lax.Precision.HIGHEST)
    coulomb = jnp.zeros((N, N), jnp.float32)
    for aux_index in range(NAUX):
        coulomb = coulomb + fit_coef[aux_index] * slab[aux_index].astype(jnp.float32)
    half_flat = jnp.transpose(half_done, (1, 0, 2)).reshape(N, NAUX * NOCC)
    exchange_mat = lax.dot_general(half_flat, half_flat, (((1,), (1,)), ((), ())), preferred_element_type=jnp.float32)
    return hcore + 2.0 * coulomb - exchange_mat
```

```python
import jax
import jax.numpy as jnp
from jax import lax
from jax.experimental.layout import Layout, with_layout_constraint
from jax.sharding import PartitionSpec as P

CHUNKS = 4


def by_rows(array):
    return with_layout_constraint(array, Layout(major_to_minor=tuple(range(array.ndim))))


def spans(row_count, chunks):
    step = -(-row_count // chunks)
    step = -(-step // 128) * 128
    return [(low, min(low + step, row_count)) for low in range(0, row_count, step)]


def gather_orbitals(orbitals, group_count):
    row_count = orbitals.shape[0]
    if row_count % group_count:
        return lax.all_gather(orbitals, "dev", axis=0, tiled=True)
    share = row_count // group_count
    mine = lax.dynamic_slice_in_dim(orbitals, lax.axis_index("grp") * share, share)
    return lax.all_gather(mine, ("dev", "grp"), axis=0, tiled=True)


def build(group_count, dev_count):
    per_group = dev_count // group_count

    def shards(slab, orbitals, hcore, metric_inv):
        aux_count, row_count, full_width = slab.shape
        group_index = lax.axis_index("grp")
        coefs = gather_orbitals(orbitals, group_count)
        pieces = spans(row_count, CHUNKS)

        halves, gathered = [], []
        density = jnp.zeros((aux_count,), jnp.float32)
        for low, high in pieces:
            by_aux = [
                by_rows(jnp.dot(slab[a, low:high], coefs, preferred_element_type=jnp.float32).astype(jnp.bfloat16))
                for a in range(aux_count)
            ]
            rows = orbitals[low:high].astype(jnp.float32)
            density = density + jnp.stack([jnp.sum(h.astype(jnp.float32) * rows) for h in by_aux])
            flat = by_rows(jnp.concatenate(by_aux, axis=1))
            halves.append(flat)
            gathered.append(by_rows(lax.all_gather(flat, "dev", axis=0, tiled=True)))
        half_flat = by_rows(jnp.concatenate(halves, axis=0))

        placed = lax.dynamic_update_slice_in_dim(
            jnp.zeros((aux_count * group_count,), jnp.float32), density, group_index * aux_count, 0
        )
        density_all = lax.psum(placed, ("grp", "dev"))
        fit_coef = jnp.dot(metric_inv, density_all, precision=lax.Precision.HIGHEST)
        local_coef = 2.0 * lax.dynamic_slice_in_dim(fit_coef, group_index * aux_count, aux_count)

        blocks = []
        for d in range(dev_count):
            cols = slice(d * row_count, (d + 1) * row_count)
            blocks.append(
                by_rows(sum(local_coef[a] * slab[a, :, cols].astype(jnp.float32) for a in range(aux_count)))
            )
        coulomb = by_rows(jnp.stack(blocks))

        sums = []
        for (low, high), whole in zip(pieces, gathered):
            width = high - low
            total = None
            for k in list(range(1, group_count)) + [0]:
                target = group_index ^ k
                others = lax.dynamic_slice_in_dim(whole, target * (per_group * width), per_group * width)
                exchange = lax.dot_general(
                    half_flat,
                    others,
                    (((1,), (1,)), ((), ())),
                    preferred_element_type=jnp.float32,
                )
                direct = lax.dynamic_slice(
                    coulomb, (target * per_group, 0, low), (per_group, row_count, width)
                )
                part = jnp.concatenate([direct[t] for t in range(per_group)], axis=1) - by_rows(exchange)
                if k:
                    pairs = [(g, g ^ k) for g in range(group_count)]
                    part = lax.ppermute(by_rows(part.astype(jnp.bfloat16)), "grp", pairs).astype(jnp.float32)
                total = part if total is None else total + part
            sums.append(by_rows(total))

        columns = []
        for t in range(per_group):
            for (low, high), total in zip(pieces, sums):
                width = high - low
                columns.append(total[:, t * width : (t + 1) * width])
        return hcore + by_rows(jnp.concatenate(columns, axis=1))

    return shards


def solution(mesh):
    return jax.shard_map(
        build(mesh.shape["grp"], mesh.shape["dev"]),
        mesh=mesh,
        in_specs=(P("grp", "dev", None), P("dev", None), P("dev", "grp"), P()),
        out_specs=P("dev", "grp"),
        check_vma=False,
    )
```

```python
import jax
import jax.numpy as jnp
from jax import lax
from jax.experimental.layout import Layout, with_layout_constraint
from jax.sharding import PartitionSpec as P

CHUNKS = 4


def by_rows(array):
    return with_layout_constraint(array, Layout(major_to_minor=tuple(range(array.ndim))))


def spans(row_count, chunks):
    step = -(-row_count // chunks)
    step = -(-step // 128) * 128
    return [(low, min(low + step, row_count)) for low in range(0, row_count, step)]


def build(group_count, dev_count):
    per_group = dev_count // group_count

    def shards(slab, orbitals, hcore, metric_inv):
        aux_count, row_count, full_width = slab.shape
        group_index = lax.axis_index("grp")
        coefs = lax.all_gather(orbitals, "dev", axis=0, tiled=True)
        pieces = spans(row_count, CHUNKS)

        halves, gathered = [], []
        density = jnp.zeros((aux_count,), jnp.float32)
        for low, high in pieces:
            by_aux = [
                by_rows(jnp.dot(slab[a, low:high], coefs, preferred_element_type=jnp.float32).astype(jnp.bfloat16))
                for a in range(aux_count)
            ]
            rows = orbitals[low:high].astype(jnp.float32)
            density = density + jnp.stack([jnp.sum(h.astype(jnp.float32) * rows) for h in by_aux])
            flat = by_rows(jnp.concatenate(by_aux, axis=1))
            flat, coefs = lax.optimization_barrier((flat, coefs))
            halves.append(flat)
            gathered.append(by_rows(lax.all_gather(flat, "dev", axis=0, tiled=True)))
        half_flat = by_rows(jnp.concatenate(halves, axis=0))

        placed = lax.dynamic_update_slice_in_dim(
            jnp.zeros((aux_count * group_count,), jnp.float32), density, group_index * aux_count, 0
        )
        density_all = lax.psum(placed, ("grp", "dev"))
        fit_coef = jnp.dot(metric_inv, density_all, precision=lax.Precision.HIGHEST)
        local_coef = 2.0 * lax.dynamic_slice_in_dim(fit_coef, group_index * aux_count, aux_count)

        fock = hcore
        received = []
        for index, ((low, high), whole) in enumerate(zip(pieces, gathered)):
            width = high - low
            if index >= 2:
                *landed, local_coef = lax.optimization_barrier((*received[index - 2], local_coef))
                received[index - 2] = landed
            blocks = []
            for d in range(dev_count):
                cols = slice(d * row_count + low, d * row_count + high)
                blocks.append(
                    by_rows(sum(local_coef[a] * slab[a, :, cols].astype(jnp.float32) for a in range(aux_count)))
                )
            coulomb = by_rows(jnp.stack(blocks))
            parts = []
            for k in list(range(1, group_count)) + [0]:
                target = group_index ^ k
                others = lax.dynamic_slice_in_dim(whole, target * (per_group * width), per_group * width)
                exchange = lax.dot_general(
                    half_flat, others, (((1,), (1,)), ((), ())), preferred_element_type=jnp.float32
                )
                direct = lax.dynamic_slice_in_dim(coulomb, target * per_group, per_group)
                part = jnp.concatenate([direct[t] for t in range(per_group)], axis=1) - by_rows(exchange)
                parts.append(by_rows(part.astype(jnp.bfloat16)) if k else by_rows(part))
            *parts, local_coef = lax.optimization_barrier((*parts, local_coef))
            for k in range(1, group_count):
                pairs = [(g, g ^ k) for g in range(group_count)]
                parts[k - 1] = lax.ppermute(parts[k - 1], "grp", pairs)
            received.append(parts)
        for (low, high), parts in zip(pieces, received):
            width = high - low
            total = parts[-1]
            for part in parts[:-1]:
                total = total + part.astype(jnp.float32)
            for t in range(per_group):
                first = t * row_count + low
                block = hcore[:, first : first + width] + total[:, t * width : (t + 1) * width]
                fock = lax.dynamic_update_slice(fock, block, (0, first))
        return fock

    return shards


def solution(mesh):
    return jax.shard_map(
        build(mesh.shape["grp"], mesh.shape["dev"]),
        mesh=mesh,
        in_specs=(P("grp", "dev", None), P("dev", None), P("dev", "grp"), P()),
        out_specs=P("dev", "grp"),
        check_vma=False,
    )
```
